256 devices in a mesh: row: 4 (over x), col: 4 (over y), depth: 16 (over z, core).
Axes of the slice: x: 4, y: 4, z: 8, core: 2. Of those that a mesh axis runs over, the one named last changes fastest.
Arguments:
- three_center: bfloat16 [8192, 8192], P('col', ('row', 'depth')), may hold values from -6 to 6
- three_mask: int32 [256, 256], P('col', ('row', 'depth')), may hold values from 0 to 1, as said below
- density: bfloat16 [8192, 8192], P(('col', 'depth'), 'row'), may hold values from -0.375 to 0.375
- density_mask: int32 [256, 256], P(('col', 'depth'), 'row'), may hold values from 0 to 1, as said below
- nu_sizes: int32 [256], P(('row', 'depth')), may hold values from 5 to 32
Outputs:
- contracted: bfloat16 [8192, 8192], P('col', ('row', 'depth'))
The draws below stay inside these ranges and needn't reach their ends.
Inputs may be any that keep to these rules, and one draw needn't show every extreme that they name: `three_mask`: 1 marks an occupied tile. `density_mask`: 1 marks an occupied tile.
All inputs are finite; a program needn't handle non-finite values.
Results may differ from the reference program's by a relative error of at most 0.022.
Values may be sent and summed in bfloat16 or wider, within the bound.
No kernel may reach another device: no remote copies, remote signals or barrier semaphores. Data moves between devices by JAX's collectives and lax.ppermute only.
A program may use at most 128 MiB of HBM per device.

```python
import jax
import jax.numpy as jnp
from jax import lax

BS = 32
KB_DEV = 4
M = 8192
K = 8192
N = 8192
N_ROW = 4
N_DEPTH = 16


def draw_three_mask(key, part):
    key = jax.random.fold_in(key, 11)
    first_key, second_key = jax.random.split(key)
    limits = jax.random.randint(first_key, (M // BS, 1), 10, 95)
    rolls = jax.random.randint(second_key, (M // BS, K // BS), 0, 100)
    return (rolls < limits).astype(jnp.int32)


def draw_density_mask(key, part):
    key = jax.random.fold_in(key, 23)
    row_count = K // BS
    col_count = N // BS
    circle = row_count * col_count
    row_pos = jnp.arange(row_count, dtype=jnp.int32)[:, None] * col_count
    col_pos = jnp.arange(col_count, dtype=jnp.int32)[None, :] * row_count
    offset = (row_pos - col_pos) % circle
    distance = jnp.minimum(offset, circle - offset)
    rolls = jax.random.randint(key, (row_count, col_count), 0, 100)
    return (distance * 400 < circle * (60 + rolls)).astype(jnp.int32)


def touch_ends(drawn, own_key, low, high):
    longest = drawn.shape.index(max(drawn.shape))
    spots = []
    for shift in (0, 1):
        where = [jax.random.randint(jax.random.fold_in(own_key, axis), (), 0, length) for axis, length in enumerate(drawn.shape)]
        where[longest] = (where[longest] + shift) % drawn.shape[longest]
        spots.append(tuple(where))
    return drawn.at[spots[0]].set(low).at[spots[1]].set(high)


def with_spikes(array, rng, source, target, blocks, factor):
    def block_of(dim):
        return (jnp.arange(array.shape[dim]) // (array.shape[dim] // blocks)).reshape((-1,) + (1,) * (array.ndim - 1 - dim))

    first = jax.random.permutation(rng, blocks)[block_of(target)]
    other_side = (block_of(target) + blocks // 2) % blocks
    return jnp.where((block_of(source) == first) | (block_of(source) == other_side), factor * array, array)


def shard_levels(stream_key, dims, shards, smallest, largest):
    loudness = 1.0
    for dim, parts in shards:
        heights = jax.random.uniform(jax.random.fold_in(jax.random.fold_in(stream_key, 6), dim), (parts,), jnp.float32, smallest / len(shards), largest / len(shards))
        loudness = loudness * jnp.repeat(jnp.exp(heights), dims[dim] // parts).reshape((-1,) + (1,) * (len(dims) - 1 - dim))
    return loudness


def gaussian(rng, shape, spread, most, cuts=(), held_as=jnp.bfloat16):
    drawn = jax.random.normal(rng, shape, jnp.float32) * spread
    if len(cuts) > 0:
        drawn = shard_levels(rng, shape, cuts, -0.22, 0.18) * drawn
    return jnp.clip(drawn, min=-most, max=most).astype(held_as)


def noise_with(stream_key, shape, spread, bound, shards, heavy, held_as=jnp.bfloat16):
    drawn = spread * jax.random.normal(stream_key, shape, jnp.float32)
    if shards:
        drawn = drawn * shard_levels(stream_key, shape, shards, -0.22, 0.18)
    return jnp.clip(with_spikes(drawn, jax.random.fold_in(stream_key, 3), *heavy), -bound, bound).astype(held_as)


def setup_inputs(seed: int = 0) -> dict:
    key_list = jax.random.split(jax.random.key(seed), 6)
    three_center = gaussian(key_list[0], (M, K), 1.0, 6.0, ((0, 4), (1, 64)))
    three_mask = draw_three_mask(jax.random.fold_in(key_list[5], 71), 0)
    density = noise_with(key_list[2], (K, N), (K // 4) ** -0.5, 0.375, ((0, 64), (1, 4)), (0, 1, 64, 4.0))
    density_mask = draw_density_mask(jax.random.fold_in(key_list[5], 71), 0)
    nu_sizes = touch_ends(jax.random.randint(key_list[4], (K // BS,), 5, BS + 1), jax.random.fold_in(key_list[4], 1), 5, BS).astype(jnp.int32)
    return dict(three_center=three_center, three_mask=three_mask, density=density, density_mask=density_mask, nu_sizes=nu_sizes)


def reference(three_center, three_mask, density, density_mask, nu_sizes):
    inside = (jnp.arange(BS)[None, :] < nu_sizes[:, None]).astype(jnp.int32)
    keep_three = (three_mask[:, None, :, None] * inside[None, None, :, :]).astype(jnp.bfloat16)
    live = (three_center.reshape(M // BS, BS, K // BS, BS) * keep_three).reshape(M, K)
    keep_dens = density_mask[:, None, :, None].astype(jnp.bfloat16)
    dens = (density.reshape(K // BS, BS, N // BS, BS) * keep_dens).reshape(K, N)
    live_layers = live.reshape(M, N_ROW, N_DEPTH, KB_DEV * BS)
    dens_layers = dens.reshape(N_ROW, N_DEPTH, KB_DEV * BS, N)

    def add_layer(layer_index, total):
        left = lax.dynamic_index_in_dim(live_layers, layer_index, 2, keepdims=False)
        right = lax.dynamic_index_in_dim(dens_layers, layer_index, 1, keepdims=False)
        partial_sum = jnp.dot(left.reshape(M, N_ROW * KB_DEV * BS), right.reshape(N_ROW * KB_DEV * BS, N), preferred_element_type=jnp.float32)
        rounded = lax.optimization_barrier(partial_sum.astype(jnp.bfloat16))
        return total + rounded.astype(jnp.float32)

    product = lax.fori_loop(0, N_DEPTH, add_layer, jnp.zeros((M, N), jnp.float32))
    return product.astype(jnp.bfloat16)
```

```python
import functools

import jax
import jax.numpy as jnp
from jax import lax
from jax.experimental import pallas as pl
from jax.experimental.pallas import tpu as pltpu
from jax.sharding import PartitionSpec as P

BS = 32
CHUNKS = 2
EARLY = (4, 3, 5)
LATE = (2, 6, 1, 7, 0)
VMEM_BYTES = 32 * 1024 * 1024

vmem = functools.partial(pl.BlockSpec, memory_space=pltpu.VMEM)
smem = functools.partial(pl.BlockSpec, memory_space=pltpu.SMEM)


def call(kernel, outs, operands, in_specs, scratch=(), flops=0):
    moved = sum(a.size * a.dtype.itemsize for a in operands)
    moved += sum(o.size * o.dtype.itemsize for o in outs)
    return pl.pallas_call(
        kernel,
        out_shape=outs,
        in_specs=in_specs,
        out_specs=[vmem()] * len(outs),
        scratch_shapes=list(scratch),
        compiler_params=pltpu.CompilerParams(vmem_limit_bytes=VMEM_BYTES),
        cost_estimate=pl.CostEstimate(flops=flops, bytes_accessed=moved, transcendentals=0),
    )(*operands)


def mask_three(three_center, three_mask, nu_sizes):
    rows, cols = three_center.shape
    part = rows // CHUNKS
    tiles = part // BS

    def kernel(sizes_ref, mask_ref, three_ref, *outs):
        lane = lax.broadcasted_iota(jnp.int32, (rows // BS, cols), 1)
        size = jnp.zeros_like(lane)
        keep = jnp.zeros_like(lane)
        for j in range(cols // BS):
            here = lane // BS == j
            size = jnp.where(here, sizes_ref[j], size)
            keep = jnp.where(here, mask_ref[:, j : j + 1], keep)
        keep = jnp.where(lane % BS < size, keep, 0).astype(jnp.float32)
        for h in range(CHUNKS):
            for t in range(tiles):
                g = h * tiles + t
                wide = jnp.broadcast_to(keep[g : g + 1, :], (BS, cols)).astype(jnp.bfloat16)
                outs[h][t * BS : (t + 1) * BS, :] = three_ref[g * BS : (g + 1) * BS, :] * wide

    return call(
        kernel,
        [jax.ShapeDtypeStruct((part, cols), jnp.bfloat16)] * CHUNKS,
        (nu_sizes, three_mask, three_center),
        [smem(), vmem(), vmem()],
    )


def mask_density(place, density, density_mask):
    rows, cols = density.shape
    row_tiles, col_tiles = density_mask.shape
    share = 128
    count = cols // (2 * share)

    def kernel(place_ref, mask_ref, dens_ref, own_ref, other_ref, held):
        z, c = place_ref[0], place_ref[1]
        spread = (
            lax.broadcasted_iota(jnp.int32, (col_tiles, cols), 1) // BS
            == lax.broadcasted_iota(jnp.int32, (col_tiles, cols), 0)
        ).astype(jnp.bfloat16)
        keep = jnp.dot(
            mask_ref[...].astype(jnp.float32).astype(jnp.bfloat16), spread, preferred_element_type=jnp.float32
        )
        for i in range(row_tiles):
            wide = jnp.broadcast_to(keep[i : i + 1, :], (BS, cols)).astype(jnp.bfloat16)
            held[i * BS : (i + 1) * BS, :] = dens_ref[i * BS : (i + 1) * BS, :] * wide
        for j in range(count):
            first = lax.rem(z + j, count) * 2
            own = pl.multiple_of((first + c) * share, share)
            other = pl.multiple_of((first + 1 - c) * share, share)
            own_ref[j] = held[:, pl.ds(own, share)]
            other_ref[j] = held[:, pl.ds(other, share)]

    return call(
        kernel,
        [jax.ShapeDtypeStruct((count, rows, share), jnp.bfloat16)] * 2,
        (place, density_mask, density),
        [smem(), vmem(), vmem()],
        [pltpu.VMEM((rows, cols), jnp.bfloat16)],
        flops=2 * row_tiles * col_tiles * cols,
    )


def dots(place, three, dens, groups, kinds):
    part, deep = three[0].shape
    pieces = len(dens)
    k_piece = dens[0].shape[1]
    share = dens[0].shape[2]
    tile = 256

    def kernel(place_ref, *refs):
        a_refs, b_refs = refs[: len(three)], refs[len(three) : len(three) + pieces]
        outs = refs[len(three) + pieces : -1]
        held = refs[-1]
        turn = place_ref[2]
        for s in range(pieces):
            at = pl.multiple_of(lax.rem(s + turn, pieces) * k_piece, k_piece)
            first = 0
            for group in groups:
                for n, j in enumerate(group):
                    held[pl.ds(at, k_piece), (first + n) * share : (first + n + 1) * share] = b_refs[s][j]
                first += len(group)
        first = 0
        for group, out in zip(groups, outs):
            width = len(group) * share
            right = held[:, first * share : first * share + width]
            for m in range(0, part, tile):
                left = jnp.concatenate([a[m : m + tile, :] for a in a_refs], axis=1)
                out[m : m + tile, :] = jnp.dot(left, right, preferred_element_type=jnp.float32).astype(out.dtype)
            first += len(group)

    total = sum(len(g) for g in groups)
    return call(
        kernel,
        [jax.ShapeDtypeStruct((part, len(g) * share), kind) for g, kind in zip(groups, kinds)],
        (place, *three, *dens),
        [smem()] + [vmem()] * (len(three) + pieces),
        [pltpu.VMEM((pieces * k_piece, total * share), jnp.bfloat16)],
        flops=2 * part * deep * len(three) * total * share,
    )


def shifted(block, axis, distance):
    count = lax.axis_size(axis)
    return lax.ppermute(block, axis, [((i + distance) % count, i) for i in range(count)])


def along_z(block, distance):
    count = lax.axis_size("depth") // 2
    route = [(z * 2 + c, (z + distance) % count * 2 + c) for z in range(count) for c in range(2)]
    return lax.ppermute(block, "depth", route)


def other_core(block):
    return lax.ppermute(block, "depth", [(i, i ^ 1) for i in range(lax.axis_size("depth"))])


def gathered(block, axis):
    up, down, far = shifted(block, axis, 1), shifted(block, axis, 3), shifted(block, axis, 2)
    return [block, up, far, down]


def on_device(three_center, three_mask, density, density_mask, nu_sizes):
    row, col, depth = lax.axis_index("row"), lax.axis_index("col"), lax.axis_index("depth")
    place = jnp.stack([depth // 2, depth % 2, (col - row) % 4]).astype(jnp.int32)

    chunks = mask_three(three_center, three_mask, nu_sizes)
    own, other = mask_density(place, density, density_mask)
    arrived = other_core(other)
    both = jnp.concatenate([own, arrived], axis=1)
    early = gathered(jnp.stack([both[j] for j in EARLY]), "col")
    late = gathered(jnp.stack([both[j] for j in LATE]), "col")

    outs = []
    for chunk in chunks:
        blocks = gathered(chunk, "row")
        three = []
        for block in blocks:
            three += [block, other_core(block)]
        half = chunk.shape[0] // 2
        far, near3 = dots(place, three, early, ((0,), (1, 2)), (jnp.bfloat16, jnp.float32))
        to_right, to_left = along_z(far[:half], 1), along_z(far[half:], -1)
        near2, near1, near0 = dots(place, three, late, ((0, 1), (2, 3), (4,)), (jnp.float32,) * 3)
        share = far.shape[1]
        none = jnp.zeros((half, share), jnp.float32)
        to_right = jnp.concatenate([to_right.astype(jnp.float32), none])
        to_left = jnp.concatenate([none, to_left.astype(jnp.float32)])
        for near in (near3, near2, near1):
            to_right = along_z((near[:, :share] + to_right).astype(jnp.bfloat16), 1).astype(jnp.float32)
            to_left = along_z((near[:, share:] + to_left).astype(jnp.bfloat16), -1).astype(jnp.float32)
        outs.append((near0 + to_right + to_left).astype(jnp.bfloat16))
    return jnp.concatenate(outs)


def solution(mesh):
    in_specs = (
        P("col", ("row", "depth")),
        P("col", ("row", "depth")),
        P(("col", "depth"), "row"),
        P(("col", "depth"), "row"),
        P(("row", "depth")),
    )
    out_specs = P("col", ("row", "depth"))
    return jax.shard_map(
        on_device, mesh=mesh, in_specs=in_specs, out_specs=out_specs, check_vma=False
    )
```

```python
import functools

import jax
import jax.numpy as jnp
from jax import lax
from jax.experimental import pallas as pl
from jax.experimental.pallas import tpu as pltpu
from jax.sharding import PartitionSpec as P

BS = 32
VMEM_BYTES = 8 * 1024 * 1024

vmem = functools.partial(pl.BlockSpec, memory_space=pltpu.VMEM)
smem = functools.partial(pl.BlockSpec, memory_space=pltpu.SMEM)


def call(kernel, outs, operands, in_specs, scratch=(), flops=0, limit=VMEM_BYTES):
    moved = sum(a.size * a.dtype.itemsize for a in operands)
    moved += sum(o.size * o.dtype.itemsize for o in outs)
    return pl.pallas_call(
        kernel,
        out_shape=outs,
        in_specs=in_specs,
        out_specs=[vmem()] * len(outs),
        scratch_shapes=list(scratch),
        compiler_params=pltpu.CompilerParams(vmem_limit_bytes=limit),
        cost_estimate=pl.CostEstimate(flops=flops, bytes_accessed=moved, transcendentals=0),
    )(*operands)


def masked(three_center, three_mask, density, density_mask, nu_sizes):
    rows, cols = three_center.shape
    deep, wide = density.shape
    share = 128
    count = wide // (2 * share)
    tiles = cols // BS

    def kernel(three_hbm, mask3_hbm, dens_hbm, maskd_hbm, sizes_hbm, live_ref, own_ref, other_ref, *scratch):
        three_ref, mask3_ref, dens_ref, maskd_ref, sizes_ref, held, sems = scratch
        depth = lax.axis_index("depth")
        z, c = depth // 2, depth % 2
        copies = [
            pltpu.make_async_copy(src, dst, sems.at[i])
            for i, (src, dst) in enumerate(
                (
                    (dens_hbm, dens_ref),
                    (maskd_hbm, maskd_ref),
                    (sizes_hbm, sizes_ref),
                    (mask3_hbm, mask3_ref),
                    (three_hbm, three_ref),
                )
            )
        ]
        for copy in copies:
            copy.start()
        for copy in copies[:2]:
            copy.wait()
        lane = lax.broadcasted_iota(jnp.int32, (wide // BS, wide), 1)
        spread = (lane // BS == lax.broadcasted_iota(jnp.int32, lane.shape, 0)).astype(jnp.bfloat16)
        keep = jnp.dot(
            maskd_ref[...].astype(jnp.float32).astype(jnp.bfloat16), spread, preferred_element_type=jnp.float32
        )
        for i in range(deep // BS):
            kept = jnp.broadcast_to(keep[i : i + 1, :], (BS, wide)).astype(jnp.bfloat16)
            held[i * BS : (i + 1) * BS, :] = dens_ref[i * BS : (i + 1) * BS, :] * kept
        for j in range(count):
            first = lax.rem(z + j, count) * 2
            own_at = pl.multiple_of((first + c) * share, share)
            other_at = pl.multiple_of((first + 1 - c) * share, share)
            own_ref[j] = held[:, pl.ds(own_at, share)]
            other_ref[j] = held[:, pl.ds(other_at, share)]
        for copy in copies[2:]:
            copy.wait()
        lane = lax.broadcasted_iota(jnp.int32, (tiles, cols), 1)
        tile = lax.broadcasted_iota(jnp.int32, lane.shape, 0)
        size = jnp.zeros_like(lane)
        for j in range(tiles):
            size = jnp.where(tile == j, sizes_ref[j], size)
        spread = ((lane // BS == tile) & (lane % BS < size)).astype(jnp.bfloat16)
        keep = lax.dot_general(
            mask3_ref[...].astype(jnp.float32).astype(jnp.bfloat16),
            spread,
            (((0,), (0,)), ((), ())),
            preferred_element_type=jnp.float32,
        )
        for g in range(rows // BS):
            kept = jnp.broadcast_to(keep[g : g + 1, :], (BS, cols)).astype(jnp.bfloat16)
            live_ref[g * BS : (g + 1) * BS, :] = three_ref[g * BS : (g + 1) * BS, :] * kept

    return call(
        kernel,
        [jax.ShapeDtypeStruct((rows, cols), jnp.bfloat16)]
        + [jax.ShapeDtypeStruct((count, deep, share), jnp.bfloat16)] * 2,
        (three_center, three_mask.T, density, density_mask, nu_sizes),
        [pl.BlockSpec(memory_space=pltpu.HBM)] * 5,
        [
            pltpu.VMEM((rows, cols), jnp.bfloat16),
            pltpu.VMEM((tiles, rows // BS), jnp.int32),
            pltpu.VMEM((deep, wide), jnp.bfloat16),
            pltpu.VMEM((deep // BS, wide // BS), jnp.int32),
            pltpu.SMEM((tiles,), jnp.int32),
            pltpu.VMEM((deep, wide), jnp.bfloat16),
            pltpu.SemaphoreType.DMA((5,)),
        ],
        limit=56 * 1024 * 1024,
    )


def dots(three, dens, jobs):
    pieces = len(dens)
    k_piece, share = dens[0].shape[1:]
    tile = 256
    arrays = []
    for array, _ in three:
        if not any(array is other for other in arrays):
            arrays.append(array)
    where = [[array is other for other in arrays].index(True) for array, _ in three]
    shares = [j for _, _, picked, _ in jobs for j in picked]
    shares = sorted(set(shares), key=shares.index)

    def kernel(*refs):
        a_refs, b_refs = refs[: len(arrays)], refs[len(arrays) : len(arrays) + pieces]
        outs, held = list(refs[len(arrays) + pieces : -1]), refs[-1]
        across = lax.axis_index("col") - lax.axis_index("row")
        turn = jnp.where(lax.axis_index("depth") % 2 == 0, across, -across) + pieces
        for s in range(pieces):
            at = pl.multiple_of(lax.rem(s + turn, pieces) * k_piece, k_piece)
            for n, j in enumerate(shares):
                held[pl.ds(at, k_piece), n * share : (n + 1) * share] = b_refs[s][j]
        for first, rows, picked, wanted in jobs:
            lo = shares.index(picked[0]) * share
            right = held[:, lo : lo + len(picked) * share]
            for m in range(0, rows, tile):
                left = jnp.concatenate(
                    [a_refs[w][base + first + m : base + first + m + tile, :] for w, (_, base) in zip(where, three)],
                    axis=1,
                )
                total = jnp.dot(left, right, preferred_element_type=jnp.float32)
                for out, (kind, r0, height, c0, width) in zip(outs, wanted):
                    if r0 <= m < r0 + height:
                        out[m - r0 : m - r0 + tile, :] = total[:, c0 : c0 + width].astype(kind)
            outs = outs[len(wanted) :]

    deep = pieces * k_piece
    return call(
        kernel,
        [jax.ShapeDtypeStruct((o[2], o[4]), o[0]) for job in jobs for o in job[3]],
        (*arrays, *dens),
        [vmem()] * (len(arrays) + pieces),
        [pltpu.VMEM((deep, len(shares) * share), jnp.bfloat16)],
        flops=2 * deep * share * sum(rows * len(picked) for _, rows, picked, _ in jobs),
    )


def along_z(block, distance):
    count = lax.axis_size("depth") // 2
    route = [(z * 2 + c, (z + distance) % count * 2 + c) for z in range(count) for c in range(2)]
    return lax.ppermute(block, "depth", route)


def other_core(block):
    return lax.ppermute(block, "depth", [(i, i ^ 1) for i in range(lax.axis_size("depth"))])


def opposed(block, axis, step):
    count, depth = lax.axis_size(axis), lax.axis_size("depth")
    route = [
        (i * depth + d, (i + (step if d % 2 == 0 else -step)) % count * depth + d)
        for i in range(count)
        for d in range(depth)
    ]
    return lax.ppermute(block, (axis, "depth"), route)


def after(block, *earlier):
    return lax.optimization_barrier((block, *earlier))[0]


def on_device(three_center, three_mask, density, density_mask, nu_sizes):
    live, own, other = masked(three_center, three_mask, density, density_mask, nu_sizes)
    dens = jnp.concatenate([own, other_core(other)], axis=1)
    a_back, b_back = opposed(live, "row", 1), opposed(dens, "col", 1)
    a_front, b_front = opposed(live, "row", -1), opposed(dens, "col", -1)
    a_back, a_front, b_back, b_front = lax.optimization_barrier((a_back, a_front, b_back, b_front))
    a_far, b_far = opposed(a_back, "row", 1), opposed(b_back, "col", 1)
    live_other, front_other, back_other = other_core(live), other_core(a_front), other_core(a_back)
    far_other = other_core(a_far)
    n = live.shape[0]
    three = [(x, 0) for x in (live, live_other, a_front, back_other, a_far, far_other, a_back, front_other)]
    dens = [dens, b_front, b_far, b_back]

    share = dens[0].shape[2]
    half = n // 2
    bf16, f32 = jnp.bfloat16, jnp.float32

    def later(done):
        return [(after(live, done), 0)] + three[1:]

    def plus(near, arrived):
        return (near + arrived.astype(f32)).astype(bf16)

    def job(first, kinds, picked):
        return [(first, half, picked, [(kind, 0, half, i * share, share) for i, kind in enumerate(kinds)])]

    (ra4,) = dots(three, dens, job(0, (bf16,), (4,)))
    ra = along_z(ra4, 1)
    (lb4,) = dots(later(ra4), dens, job(half, (bf16,), (4,)))
    lb = along_z(lb4, -1)
    rb3, lb3 = dots(later(lb4), dens, job(half, (bf16, f32), (3, 5)))
    rb = along_z(rb3, 1)
    ra3, la3 = dots(later(rb3), dens, job(0, (f32, bf16), (3, 5)))
    la = along_z(la3, -1)
    ra2, la2, rb2, lb2 = dots(later(la3), dens, job(0, (f32, f32), (2, 6)) + job(half, (f32, f32), (2, 6)))
    ra, lb = along_z(plus(ra3, ra), 1), along_z(plus(lb3, lb), -1)
    ra1, la1, rb1, lb1 = dots(later(ra2), dens, job(0, (f32, f32), (1, 7)) + job(half, (f32, f32), (1, 7)))
    la, rb = along_z(plus(la2, la), -1), along_z(plus(rb2, rb), 1)
    ra, lb = along_z(plus(ra2, ra), 1), along_z(plus(lb2, lb), -1)
    (end,) = dots(later(ra1), dens, [(0, n, (0,), [(f32, 0, n, 0, share)])])
    la, rb = along_z(plus(la1, la), -1), along_z(plus(rb1, rb), 1)
    ra, lb = along_z(plus(ra1, ra), 1), along_z(plus(lb1, lb), -1)
    top = end[:half] + la.astype(f32) + ra.astype(f32)
    bottom = end[half:] + rb.astype(f32) + lb.astype(f32)
    return jnp.concatenate([top.astype(bf16), bottom.astype(bf16)])


def solution(mesh):
    in_specs = (
        P("col", ("row", "depth")),
        P("col", ("row", "depth")),
        P(("col", "depth"), "row"),
        P(("col", "depth"), "row"),
        P(("row", "depth")),
    )
    out_specs = P("col", ("row", "depth"))
    return jax.shard_map(
        on_device, mesh=mesh, in_specs=in_specs, out_specs=out_specs, check_vma=False
    )
```

```python
import functools

import jax
import jax.numpy as jnp
from jax import lax
from jax.experimental import pallas as pl
from jax.experimental.pallas import tpu as pltpu
from jax.sharding import PartitionSpec as P

BS = 32
EARLY = (4, 3, 5)
LATE = (2, 6, 1, 7, 0)
COST = 1
VMEM_BYTES = 8 * 1024 * 1024

vmem = functools.partial(pl.BlockSpec, memory_space=pltpu.VMEM)
smem = functools.partial(pl.BlockSpec, memory_space=pltpu.SMEM)


def call(kernel, outs, operands, in_specs, scratch=(), flops=0, moved=0, limit=VMEM_BYTES):
    return pl.pallas_call(
        kernel,
        out_shape=outs,
        in_specs=in_specs,
        out_specs=[vmem()] * len(outs),
        scratch_shapes=list(scratch),
        compiler_params=pltpu.CompilerParams(vmem_limit_bytes=limit),
        cost_estimate=pl.CostEstimate(flops=flops, bytes_accessed=moved, transcendentals=0),
    )(*operands)


def masked(three_center, three_mask, density, density_mask, nu_sizes):
    rows, cols = three_center.shape
    deep, wide = density.shape
    share = 128
    count = wide // (2 * share)
    tiles = cols // BS

    def kernel(three_hbm, mask3_hbm, dens_hbm, maskd_hbm, sizes_hbm, live_ref, cut_ref, swap_ref, *scratch):
        three_ref, mask3_ref, dens_ref, maskd_ref, sizes_ref, held, sems = scratch
        depth = lax.axis_index("depth")
        z, c = depth // 2, depth % 2
        copies = [
            pltpu.make_async_copy(src, dst, sems.at[i])
            for i, (src, dst) in enumerate(
                (
                    (dens_hbm, dens_ref),
                    (maskd_hbm, maskd_ref),
                    (sizes_hbm, sizes_ref),
                    (mask3_hbm, mask3_ref),
                    (three_hbm, three_ref),
                )
            )
        ]
        for copy in copies:
            copy.start()
        for copy in copies[:2]:
            copy.wait()
        lane = lax.broadcasted_iota(jnp.int32, (wide // BS, wide), 1)
        spread = (lane // BS == lax.broadcasted_iota(jnp.int32, lane.shape, 0)).astype(jnp.bfloat16)
        keep = jnp.dot(
            maskd_ref[...].astype(jnp.float32).astype(jnp.bfloat16), spread, preferred_element_type=jnp.float32
        )
        for i in range(deep // BS):
            kept = jnp.broadcast_to(keep[i : i + 1, :], (BS, wide)).astype(jnp.bfloat16)
            held[i * BS : (i + 1) * BS, :] = dens_ref[i * BS : (i + 1) * BS, :] * kept
        at, swap_at = 0, rows
        for shares in (EARLY, LATE):
            for side in (0, 1):
                for j in shares:
                    here = lax.rem(z + j, count) * 2 + (c if side == 0 else 1 - c)
                    piece = held[:, pl.ds(pl.multiple_of(here * share, share), share)]
                    cut_ref[at : at + deep, :] = piece
                    at += deep
                    if side:
                        swap_ref[swap_at : swap_at + deep, :] = piece
                        swap_at += deep
        for copy in copies[2:]:
            copy.wait()
        lane = lax.broadcasted_iota(jnp.int32, (tiles, cols), 1)
        tile = lax.broadcasted_iota(jnp.int32, lane.shape, 0)
        size = jnp.zeros_like(lane)
        for j in range(tiles):
            size = jnp.where(tile == j, sizes_ref[j], size)
        spread = ((lane // BS == tile) & (lane % BS < size)).astype(jnp.bfloat16)
        keep = lax.dot_general(
            mask3_ref[...].astype(jnp.float32).astype(jnp.bfloat16),
            spread,
            (((0,), (0,)), ((), ())),
            preferred_element_type=jnp.float32,
        )
        for g in range(rows // BS):
            kept = jnp.broadcast_to(keep[g : g + 1, :], (BS, cols)).astype(jnp.bfloat16)
            tile_rows = three_ref[g * BS : (g + 1) * BS, :] * kept
            live_ref[g * BS : (g + 1) * BS, :] = tile_rows
            swap_ref[g * BS : (g + 1) * BS, :] = tile_rows

    return call(
        kernel,
        [jax.ShapeDtypeStruct((rows, cols), jnp.bfloat16)]
        + [jax.ShapeDtypeStruct((r, share), jnp.bfloat16) for r in (2 * count * deep, rows + count * deep)],
        (three_center, three_mask.T, density, density_mask, nu_sizes),
        [pl.BlockSpec(memory_space=pltpu.HBM)] * 5,
        [
            pltpu.VMEM((rows, cols), jnp.bfloat16),
            pltpu.VMEM((tiles, rows // BS), jnp.int32),
            pltpu.VMEM((deep, wide), jnp.bfloat16),
            pltpu.VMEM((deep // BS, wide // BS), jnp.int32),
            pltpu.SMEM((tiles,), jnp.int32),
            pltpu.VMEM((deep, wide), jnp.bfloat16),
            pltpu.SemaphoreType.DMA((5,)),
        ],
        limit=56 * 1024 * 1024,
    )


def dots(three, dens, jobs, cost=0):
    deep, share = 128, dens[0][0].shape[1]
    tile = 256
    arrays = []
    for array, _ in (*three, *dens):
        if not any(array is other for other in arrays):
            arrays.append(array)

    def place(array):
        return [array is other for other in arrays].index(True)

    three_at = [(place(array), base) for array, base in three]
    dens_at = [(place(array), rows) for array, rows in dens]
    shares = [j for _, picked, _ in jobs for j in picked]

    def kernel(*refs):
        ins, outs, held = refs[: len(arrays)], list(refs[len(arrays) : -1]), refs[-1]
        across = lax.axis_index("col") - lax.axis_index("row")
        turn = jnp.where(lax.axis_index("depth") % 2 == 0, across, -across) + 4
        for s, (w, rows) in enumerate(dens_at):
            at = pl.multiple_of(lax.rem(s // 2 + turn, 4) * (2 * deep) + s % 2 * deep, deep)
            for n, j in enumerate(shares):
                held[pl.ds(at, deep), n * share : (n + 1) * share] = ins[w][rows[j] : rows[j] + deep, :]
        lo = 0
        for rows, picked, kinds in jobs:
            right = held[:, lo : lo + len(picked) * share]
            lo += len(picked) * share
            for m in range(0, rows, tile):
                left = jnp.concatenate([ins[w][base + m : base + m + tile, :] for w, base in three_at], axis=1)
                total = jnp.dot(left, right, preferred_element_type=jnp.float32)
                for i, kind in enumerate(kinds):
                    outs[i][m : m + tile, :] = total[:, i * share : (i + 1) * share].astype(kind)
            outs = outs[len(kinds) :]

    return call(
        kernel,
        [jax.ShapeDtypeStruct((rows, share), kind) for rows, _, kinds in jobs for kind in kinds],
        arrays,
        [vmem()] * len(arrays),
        [pltpu.VMEM((len(dens) * deep, len(shares) * share), jnp.bfloat16)],
        flops=cost * 2 * len(dens) * deep * share * sum(rows * len(picked) for rows, picked, _ in jobs),
    )


def along_z(block, distance):
    count = lax.axis_size("depth") // 2
    route = [(z * 2 + c, (z + distance) % count * 2 + c) for z in range(count) for c in range(2)]
    return lax.ppermute(block, "depth", route)


def other_core(block):
    return lax.ppermute(block, "depth", [(i, i ^ 1) for i in range(lax.axis_size("depth"))])


def opposed(block, axis, step):
    count, depth = lax.axis_size(axis), lax.axis_size("depth")
    route = [
        (i * depth + d, (i + (step if d % 2 == 0 else -step)) % count * depth + d)
        for i in range(count)
        for d in range(depth)
    ]
    return lax.ppermute(block, (axis, "depth"), route)


def after(block, *earlier):
    return lax.optimization_barrier((block, *earlier))[0]


def on_device(three_center, three_mask, density, density_mask, nu_sizes):
    live, dens, here = masked(three_center, three_mask, density, density_mask, nu_sizes)
    bf16, f32 = jnp.bfloat16, jnp.float32
    n, deep = live.shape[0], 128
    half = n // 2
    e, l = len(EARLY) * deep, len(LATE) * deep

    def for_other(block):
        return [block[e : 2 * e], block[2 * e + l :]]

    a_back, b_back = opposed(live, "row", 1), opposed(dens, "col", 1)
    a_front, b_front = opposed(live, "row", -1), opposed(dens, "col", -1)
    here_other = other_core(here)
    a_far, b_far = opposed(a_back, "row", 1), opposed(b_back, "col", 1)
    back_other = other_core(jnp.concatenate([a_back, *for_other(b_back)]))
    a_front, b_front, here_other = lax.optimization_barrier((a_front, b_front, here_other))
    front_other = other_core(jnp.concatenate([a_front, *for_other(b_front)]))
    far_other = other_core(jnp.concatenate([a_far, *for_other(b_far)]))

    def three(at):
        return [
            (x, at) for x in (live, here_other, a_front, back_other, a_far, far_other, a_back, front_other)
        ]

    def rows(shares, at):
        return {j: at + i * deep for i, j in enumerate(shares)}

    def shares_of(shares, at, other_at):
        return [
            (x, rows(shares, at) if i % 2 == 0 else rows(shares, n + other_at))
            for i, x in enumerate((dens, here_other, b_front, back_other, b_far, far_other, b_back, front_other))
        ]

    three_a, three_b = three(0), three(half)
    dens_e, dens_l = shares_of(EARLY, 0, 0), shares_of(LATE, 2 * e, e)

    def later(pieces, done):
        held = after(pieces[0][0], done)
        return [(held, pieces[0][1])] + pieces[1:]

    def plus(near, arrived):
        return (near + arrived.astype(f32)).astype(bf16)

    (lb4,) = dots(three_b, dens_e, [(half, (4,), (bf16,))], COST)
    lb = along_z(lb4, -1)
    (ra4,) = dots(later(three_a, lb4), dens_e, [(half, (4,), (bf16,))], COST)
    ra = along_z(ra4, 1)
    la3, ra3 = dots(later(three_a, ra4), dens_e, [(half, (5, 3), (bf16, f32))], COST)
    la = along_z(la3, -1)
    rb3, lb3 = dots(later(three_b, la3), dens_e, [(half, (3, 5), (bf16, f32))], COST)
    rb = along_z(rb3, 1)
    sa = plus(ra3, ra)
    sb = plus(lb3, lb)
    ra, lb = along_z(sa, 1), along_z(sb, -1)
    ra2, la2 = dots(later(three_a, sa), dens_l, [(half, (2, 6), (f32, f32))])
    rb2, lb2 = dots(later(three_b, sb), dens_l, [(half, (2, 6), (f32, f32))])
    la, rb = along_z(plus(la2, la), -1), along_z(plus(rb2, rb), 1)
    sa = plus(ra2, ra)
    sb = plus(lb2, lb)
    ra, lb = along_z(sa, 1), along_z(sb, -1)
    ra1, la1 = dots(later(three_a, sa), dens_l, [(half, (1, 7), (f32, f32))])
    rb1, lb1 = dots(later(three_b, sb), dens_l, [(half, (1, 7), (f32, f32))])
    la, rb = along_z(plus(la1, la), -1), along_z(plus(rb1, rb), 1)
    sa = plus(ra1, ra)
    sb = plus(lb1, lb)
    ra, lb = along_z(sa, 1), along_z(sb, -1)
    (enda,) = dots(later(three_a, sa), dens_l, [(half, (0,), (f32,))])
    (endb,) = dots(later(three_b, sb), dens_l, [(half, (0,), (f32,))])
    top = enda + la.astype(f32) + ra.astype(f32)
    bottom = endb + rb.astype(f32) + lb.astype(f32)
    return jnp.concatenate([top.astype(bf16), bottom.astype(bf16)])


def solution(mesh):
    in_specs = (
        P("col", ("row", "depth")),
        P("col", ("row", "depth")),
        P(("col", "depth"), "row"),
        P(("col", "depth"), "row"),
        P(("row", "depth")),
    )
    out_specs = P("col", ("row", "depth"))
    return jax.shard_map(
        on_device, mesh=mesh, in_specs=in_specs, out_specs=out_specs, check_vma=False
    )
```

```python
import functools

import jax
import jax.numpy as jnp
from jax import lax
from jax.experimental import pallas as pl
from jax.experimental.pallas import tpu as pltpu
from jax.sharding import PartitionSpec as P

BS = 32
COST = 1
AHEAD = 2 * 10**9
VMEM_BYTES = 8 * 1024 * 1024

vmem = functools.partial(pl.BlockSpec, memory_space=pltpu.VMEM)
smem = functools.partial(pl.BlockSpec, memory_space=pltpu.SMEM)


def call(kernel, outs, operands, in_specs, scratch=(), flops=0, limit=VMEM_BYTES):
    return pl.pallas_call(
        kernel,
        out_shape=outs,
        in_specs=in_specs,
        out_specs=[vmem()] * len(outs),
        scratch_shapes=list(scratch),
        compiler_params=pltpu.CompilerParams(vmem_limit_bytes=limit),
        cost_estimate=pl.CostEstimate(flops=flops, bytes_accessed=0, transcendentals=0),
    )(*operands)


def masked(three_center, three_mask, density, density_mask, nu_sizes):
    rows, cols = three_center.shape
    deep, wide = density.shape
    share = 128
    count = wide // (2 * share)
    tiles = cols // BS

    def kernel(three_hbm, mask3_hbm, dens_hbm, maskd_hbm, sizes_hbm, live_ref, own_ref, other_ref, *scratch):
        three_ref, mask3_ref, dens_ref, maskd_ref, sizes_ref, held, sems = scratch
        depth = lax.axis_index("depth")
        z, c = depth // 2, depth % 2
        copies = [
            pltpu.make_async_copy(src, dst, sems.at[i])
            for i, (src, dst) in enumerate(
                (
                    (dens_hbm, dens_ref),
                    (maskd_hbm, maskd_ref),
                    (sizes_hbm, sizes_ref),
                    (mask3_hbm, mask3_ref),
                    (three_hbm, three_ref),
                )
            )
        ]
        for copy in copies:
            copy.start()
        for copy in copies[:2]:
            copy.wait()
        lane = lax.broadcasted_iota(jnp.int32, (wide // BS, wide), 1)
        spread = (lane // BS == lax.broadcasted_iota(jnp.int32, lane.shape, 0)).astype(jnp.bfloat16)
        keep = jnp.dot(
            maskd_ref[...].astype(jnp.float32).astype(jnp.bfloat16), spread, preferred_element_type=jnp.float32
        )
        for i in range(deep // BS):
            kept = jnp.broadcast_to(keep[i : i + 1, :], (BS, wide)).astype(jnp.bfloat16)
            held[i * BS : (i + 1) * BS, :] = dens_ref[i * BS : (i + 1) * BS, :] * kept
        for j in range(count):
            first = lax.rem(z + j, count) * 2
            for side, out_ref in ((c, own_ref), (1 - c, other_ref)):
                place = pl.multiple_of((first + side) * share, share)
                out_ref[j * deep : (j + 1) * deep, :] = held[:, pl.ds(place, share)]
        for copy in copies[2:]:
            copy.wait()
        lane = lax.broadcasted_iota(jnp.int32, (tiles, cols), 1)
        tile = lax.broadcasted_iota(jnp.int32, lane.shape, 0)
        size = jnp.zeros_like(lane)
        for j in range(tiles):
            size = jnp.where(tile == j, sizes_ref[j], size)
        spread = ((lane // BS == tile) & (lane % BS < size)).astype(jnp.bfloat16)
        keep = lax.dot_general(
            mask3_ref[...].astype(jnp.float32).astype(jnp.bfloat16),
            spread,
            (((0,), (0,)), ((), ())),
            preferred_element_type=jnp.float32,
        )
        for g in range(rows // BS):
            kept = jnp.broadcast_to(keep[g : g + 1, :], (BS, cols)).astype(jnp.bfloat16)
            live_ref[g * BS : (g + 1) * BS, :] = three_ref[g * BS : (g + 1) * BS, :] * kept

    return call(
        kernel,
        [jax.ShapeDtypeStruct((rows, cols), jnp.bfloat16)]
        + [jax.ShapeDtypeStruct((r, share), jnp.bfloat16) for r in (count * deep, count * deep)],
        (three_center, three_mask.T, density, density_mask, nu_sizes),
        [pl.BlockSpec(memory_space=pltpu.HBM)] * 5,
        [
            pltpu.VMEM((rows, cols), jnp.bfloat16),
            pltpu.VMEM((tiles, rows // BS), jnp.int32),
            pltpu.VMEM((deep, wide), jnp.bfloat16),
            pltpu.VMEM((deep // BS, wide // BS), jnp.int32),
            pltpu.SMEM((tiles,), jnp.int32),
            pltpu.VMEM((deep, wide), jnp.bfloat16),
            pltpu.SemaphoreType.DMA((5,)),
        ],
        limit=56 * 1024 * 1024,
    )


def in_order(blocks):
    deep, share = 128, blocks[0].shape[1]
    both = blocks[0].shape[0] // 2
    whole = 2 * len(blocks) * deep

    def kernel(*refs):
        out = refs[-1]
        across = lax.axis_index("col") - lax.axis_index("row")
        turn = jnp.where(lax.axis_index("depth") % 2 == 0, across, -across) + 4
        for s, block in enumerate(refs[:-1]):
            at = pl.multiple_of(lax.rem(s + turn, 4) * (2 * deep), 2 * deep)
            for j in range(both // deep):
                for side in range(2):
                    piece = block[side * both + j * deep : side * both + (j + 1) * deep, :]
                    out[pl.ds(j * whole + side * deep + at, deep), :] = piece

    return call(
        kernel,
        [jax.ShapeDtypeStruct((both // deep * whole, share), blocks[0].dtype)],
        blocks,
        [vmem()] * len(blocks),
        flops=AHEAD,
    )[0]


def dots(three, dens, jobs, cost=0):
    deep, share = 8 * 128, dens.shape[1]
    tile = 256
    arrays = []
    for array, _ in three:
        if not any(array is other for other in arrays):
            arrays.append(array)
    three_at = [([array is other for other in arrays].index(True), base) for array, base in three]

    def kernel(*refs):
        ins, dens_ref, outs = refs[: len(arrays)], refs[len(arrays)], list(refs[len(arrays) + 1 :])
        for rows, picked, kinds in jobs:
            right = jnp.concatenate([dens_ref[j * deep : (j + 1) * deep, :] for j in picked], axis=1)
            for m in range(0, rows, tile):
                left = jnp.concatenate([ins[w][base + m : base + m + tile, :] for w, base in three_at], axis=1)
                total = jnp.dot(left, right, preferred_element_type=jnp.float32)
                for i, kind in enumerate(kinds):
                    outs[i][m : m + tile, :] = total[:, i * share : (i + 1) * share].astype(kind)
            outs = outs[len(kinds) :]

    return call(
        kernel,
        [jax.ShapeDtypeStruct((rows, share), kind) for rows, _, kinds in jobs for kind in kinds],
        (*arrays, dens),
        [vmem()] * (len(arrays) + 1),
        flops=cost * 2 * deep * share * sum(rows * len(picked) for rows, picked, _ in jobs),
    )


def along_z(block, distance):
    count = lax.axis_size("depth") // 2
    route = [(z * 2 + c, (z + distance) % count * 2 + c) for z in range(count) for c in range(2)]
    return lax.ppermute(block, "depth", route)


def other_core(block):
    return lax.ppermute(block, "depth", [(i, i ^ 1) for i in range(lax.axis_size("depth"))])


def opposed(block, axis, step):
    count, depth = lax.axis_size(axis), lax.axis_size("depth")
    route = [
        (i * depth + d, (i + (step if d % 2 == 0 else -step)) % count * depth + d)
        for i in range(count)
        for d in range(depth)
    ]
    return lax.ppermute(block, (axis, "depth"), route)


def after(block, *earlier):
    return lax.optimization_barrier((block, *earlier))[0]


def on_device(three_center, three_mask, density, density_mask, nu_sizes):
    live, own, other = masked(three_center, three_mask, density, density_mask, nu_sizes)
    bf16, f32 = jnp.bfloat16, jnp.float32
    n, deep = live.shape[0], 128
    half, both = n // 2, own.shape[0]

    a_back = opposed(live, "row", 1)
    dens = jnp.concatenate([own, other_core(other)])
    b_back = opposed(dens, "col", 1)
    a_front, b_front = opposed(live, "row", -1), opposed(dens, "col", -1)
    live_other = other_core(live)
    a_far, b_far = opposed(a_back, "row", 1), opposed(b_back, "col", 1)
    back_other = other_core(a_back)
    a_front, b_front, live_other = lax.optimization_barrier((a_front, b_front, live_other))
    front_other = other_core(a_front)
    far_other = other_core(a_far)

    def three(at):
        return [
            (x, at) for x in (live, live_other, a_front, back_other, a_far, far_other, a_back, front_other)
        ]

    three_a, three_b = three(0), three(half)
    dens = in_order((dens, b_front, b_far, b_back))

    def later(pieces, done):
        held = after(pieces[0][0], done)
        return [(held, pieces[0][1])] + pieces[1:]

    def plus(near, arrived):
        return (near + arrived.astype(f32)).astype(bf16)

    (lb4,) = dots(three_b, dens, [(half, (4,), (bf16,))], COST)
    lb = along_z(lb4, -1)
    (ra4,) = dots(later(three_a, lb4), dens, [(half, (4,), (bf16,))], COST)
    ra = along_z(ra4, 1)
    la3, ra3 = dots(later(three_a, ra4), dens, [(half, (5, 3), (bf16, f32))], COST)
    la = along_z(la3, -1)
    rb3, lb3 = dots(later(three_b, la3), dens, [(half, (3, 5), (bf16, f32))], COST)
    rb = along_z(rb3, 1)
    sa = plus(ra3, ra)
    sb = plus(lb3, lb)
    ra, lb = along_z(sa, 1), along_z(sb, -1)
    ra2, la2 = dots(later(three_a, sa), dens, [(half, (2, 6), (f32, f32))])
    rb2, lb2 = dots(later(three_b, sb), dens, [(half, (2, 6), (f32, f32))])
    la, rb = along_z(plus(la2, la), -1), along_z(plus(rb2, rb), 1)
    sa = plus(ra2, ra)
    sb = plus(lb2, lb)
    ra, lb = along_z(sa, 1), along_z(sb, -1)
    ra1, la1 = dots(later(three_a, sa), dens, [(half, (1, 7), (f32, f32))])
    rb1, lb1 = dots(later(three_b, sb), dens, [(half, (1, 7), (f32, f32))])
    la, rb = along_z(plus(la1, la), -1), along_z(plus(rb1, rb), 1)
    sa = plus(ra1, ra)
    sb = plus(lb1, lb)
    ra, lb = along_z(sa, 1), along_z(sb, -1)
    (enda,) = dots(later(three_a, sa), dens, [(half, (0,), (f32,))])
    (endb,) = dots(later(three_b, sb), dens, [(half, (0,), (f32,))])
    top = enda + la.astype(f32) + ra.astype(f32)
    bottom = endb + rb.astype(f32) + lb.astype(f32)
    return jnp.concatenate([top.astype(bf16), bottom.astype(bf16)])


def solution(mesh):
    in_specs = (
        P("col", ("row", "depth")),
        P("col", ("row", "depth")),
        P(("col", "depth"), "row"),
        P(("col", "depth"), "row"),
        P(("row", "depth")),
    )
    out_specs = P("col", ("row", "depth"))
    return jax.shard_map(
        on_device, mesh=mesh, in_specs=in_specs, out_specs=out_specs, check_vma=False
    )
```

```python
import functools

import jax
import jax.numpy as jnp
from jax import lax
from jax.experimental import pallas as pl
from jax.experimental.pallas import tpu as pltpu
from jax.sharding import PartitionSpec as P

BS = 32
COST = 1
AHEAD = 2 * 10**9
VMEM_BYTES = 8 * 1024 * 1024

vmem = functools.partial(pl.BlockSpec, memory_space=pltpu.VMEM)


def call(kernel, outs, operands, in_specs, scratch=(), flops=0, limit=VMEM_BYTES, out_space=pltpu.VMEM):
    return pl.pallas_call(
        kernel,
        out_shape=outs,
        in_specs=in_specs,
        out_specs=[pl.BlockSpec(memory_space=out_space)] * len(outs),
        scratch_shapes=list(scratch),
        compiler_params=pltpu.CompilerParams(vmem_limit_bytes=limit),
        cost_estimate=pl.CostEstimate(flops=flops, bytes_accessed=0, transcendentals=0),
    )(*operands)


def masked(three_center, three_mask, density, density_mask, nu_sizes):
    rows, cols = three_center.shape
    deep, wide = density.shape
    share = 128
    count = wide // (2 * share)
    tiles = cols // BS

    def kernel(three_hbm, mask3_hbm, dens_hbm, maskd_hbm, sizes_hbm, live_hbm, own_hbm, other_hbm, *scratch):
        three_ref, mask3_ref, dens_ref, maskd_ref, sizes_ref, held, live_ref, own_ref, other_ref, sems = scratch
        depth = lax.axis_index("depth")
        z, c = depth // 2, depth % 2
        copies = [
            pltpu.make_async_copy(src, dst, sems.at[i])
            for i, (src, dst) in enumerate(
                (
                    (maskd_hbm, maskd_ref),
                    (sizes_hbm, sizes_ref),
                    (mask3_hbm, mask3_ref),
                    (dens_hbm, dens_ref),
                    (three_hbm, three_ref),
                )
            )
        ]
        for copy in copies:
            copy.start()
        lane = lax.broadcasted_iota(jnp.int32, (wide // BS, wide), 1)
        spread = (lane // BS == lax.broadcasted_iota(jnp.int32, lane.shape, 0)).astype(jnp.bfloat16)
        copies[0].wait()
        held[...] = jnp.dot(
            maskd_ref[...].astype(jnp.float32).astype(jnp.bfloat16), spread, preferred_element_type=jnp.float32
        )
        copies[1].wait()
        lane = lax.broadcasted_iota(jnp.int32, (tiles, cols), 1)
        tile = lax.broadcasted_iota(jnp.int32, lane.shape, 0)
        size = jnp.zeros_like(lane)
        for j in range(tiles):
            size = jnp.where(tile == j, sizes_ref[j], size)
        spread = ((lane // BS == tile) & (lane % BS < size)).astype(jnp.bfloat16)
        copies[2].wait()
        keep = lax.dot_general(
            mask3_ref[...].astype(jnp.float32).astype(jnp.bfloat16),
            spread,
            (((0,), (0,)), ((), ())),
            preferred_element_type=jnp.float32,
        )
        copies[3].wait()
        for j in range(count):
            first = lax.rem(z + j, count) * 2
            for side, out_ref in ((c, own_ref), (1 - c, other_ref)):
                place = pl.multiple_of((first + side) * share, share)
                for i in range(deep // BS):
                    kept = jnp.broadcast_to(held[i : i + 1, pl.ds(place, share)], (BS, share)).astype(jnp.bfloat16)
                    piece = dens_ref[i * BS : (i + 1) * BS, pl.ds(place, share)]
                    out_ref[j * deep + i * BS : j * deep + (i + 1) * BS, :] = piece * kept
        leaving = [(other_ref, other_hbm), (own_ref, own_hbm)]
        leaving = [pltpu.make_async_copy(src, dst, sems.at[5 + i]) for i, (src, dst) in enumerate(leaving)]
        for copy in leaving:
            copy.start()
        copies[4].wait()
        part = rows // 2
        for g in range(rows // BS):
            kept = jnp.broadcast_to(keep[g : g + 1, :], (BS, cols)).astype(jnp.bfloat16)
            live_ref[g * BS : (g + 1) * BS, :] = three_ref[g * BS : (g + 1) * BS, :] * kept
            if (g + 1) * BS % part == 0:
                at = pl.ds((g + 1) * BS - part, part)
                copy = pltpu.make_async_copy(live_ref.at[at], live_hbm.at[at], sems.at[6 + (g + 1) * BS // part])
                copy.start()
                leaving.append(copy)
        for copy in leaving:
            copy.wait()

    return call(
        kernel,
        [jax.ShapeDtypeStruct((rows, cols), jnp.bfloat16)]
        + [jax.ShapeDtypeStruct((r, share), jnp.bfloat16) for r in (count * deep, count * deep)],
        (three_center, three_mask.T, density, density_mask, nu_sizes),
        [pl.BlockSpec(memory_space=pltpu.HBM)] * 5,
        [
            pltpu.VMEM((rows, cols), jnp.bfloat16),
            pltpu.VMEM((tiles, rows // BS), jnp.int32),
            pltpu.VMEM((deep, wide), jnp.bfloat16),
            pltpu.VMEM((deep // BS, wide // BS), jnp.int32),
            pltpu.SMEM((tiles,), jnp.int32),
            pltpu.VMEM((deep // BS, wide), jnp.float32),
            pltpu.VMEM((rows, cols), jnp.bfloat16),
            pltpu.VMEM((count * deep, share), jnp.bfloat16),
            pltpu.VMEM((count * deep, share), jnp.bfloat16),
            pltpu.SemaphoreType.DMA((9,)),
        ],
        limit=56 * 1024 * 1024,
        out_space=pltpu.HBM,
    )


def in_order(blocks):
    deep, share = 128, blocks[0].shape[1]
    both = blocks[0].shape[0] // 2
    whole = 2 * len(blocks) * deep

    def kernel(*refs):
        out = refs[-1]
        across = lax.axis_index("col") - lax.axis_index("row")
        turn = jnp.where(lax.axis_index("depth") % 2 == 0, across, -across) + 4
        for s, block in enumerate(refs[:-1]):
            at = pl.multiple_of(lax.rem(s + turn, 4) * (2 * deep), 2 * deep)
            for j in range(both // deep):
                for side in range(2):
                    piece = block[side * both + j * deep : side * both + (j + 1) * deep, :]
                    out[pl.ds(j * whole + side * deep + at, deep), :] = piece

    return call(
        kernel,
        [jax.ShapeDtypeStruct((both // deep * whole, share), blocks[0].dtype)],
        blocks,
        [vmem()] * len(blocks),
        flops=AHEAD,
    )[0]


def dots(three, dens, jobs, cost=0):
    deep, share = 8 * 128, dens.shape[1]
    arrays = []
    for array, _ in three:
        if not any(array is other for other in arrays):
            arrays.append(array)
    three_at = [([array is other for other in arrays].index(True), base) for array, base in three]

    def kernel(*refs):
        ins, dens_ref, outs = refs[: len(arrays)], refs[len(arrays)], list(refs[len(arrays) + 1 :])
        for rows, picked, kinds in jobs:
            right = jnp.concatenate([dens_ref[j * deep : (j + 1) * deep, :] for j in picked], axis=1)
            tile = rows // -(-rows // 512)
            for m in range(0, rows, tile):
                left = jnp.concatenate([ins[w][base + m : base + m + tile, :] for w, base in three_at], axis=1)
                total = jnp.dot(left, right, preferred_element_type=jnp.float32)
                for i, kind in enumerate(kinds):
                    outs[i][m : m + tile, :] = total[:, i * share : (i + 1) * share].astype(kind)
            outs = outs[len(kinds) :]

    return call(
        kernel,
        [jax.ShapeDtypeStruct((rows, share), kind) for rows, _, kinds in jobs for kind in kinds],
        (*arrays, dens),
        [vmem()] * (len(arrays) + 1),
        flops=cost * 2 * deep * share * sum(rows * len(picked) for rows, picked, _ in jobs),
    )


def along_z(block, distance):
    count = lax.axis_size("depth") // 2
    route = [(z * 2 + c, (z + distance) % count * 2 + c) for z in range(count) for c in range(2)]
    return lax.ppermute(block, "depth", route)


def other_core(block):
    return lax.ppermute(block, "depth", [(i, i ^ 1) for i in range(lax.axis_size("depth"))])


def opposed(block, axis, step):
    count, depth = lax.axis_size(axis), lax.axis_size("depth")
    route = [
        (i * depth + d, (i + (step if d % 2 == 0 else -step)) % count * depth + d)
        for i in range(count)
        for d in range(depth)
    ]
    return lax.ppermute(block, (axis, "depth"), route)


def after(block, *earlier):
    return lax.optimization_barrier((block, *earlier))[0]


def on_device(three_center, three_mask, density, density_mask, nu_sizes):
    live, own, other = masked(three_center, three_mask, density, density_mask, nu_sizes)
    bf16, f32 = jnp.bfloat16, jnp.float32
    n, deep = live.shape[0], 128
    rows_a = n * 16 // 32
    rows_b = n - rows_a

    a_back = opposed(live, "row", 1)
    dens = jnp.concatenate([own, other_core(other)])
    b_back = opposed(dens, "col", 1)
    a_front, b_front = opposed(live, "row", -1), opposed(dens, "col", -1)
    live_other = other_core(live)
    a_far, b_far = opposed(a_back, "row", 1), opposed(b_back, "col", 1)
    back_other = other_core(a_back)
    a_front, b_front, live_other = lax.optimization_barrier((a_front, b_front, live_other))
    front_other = other_core(a_front)
    far_other = other_core(a_far)

    def three(at):
        return [
            (x, at) for x in (live, live_other, a_front, back_other, a_far, far_other, a_back, front_other)
        ]

    three_a, three_b = three(0), three(rows_a)
    dens = in_order((dens, b_front, b_far, b_back))

    def later(pieces, done):
        held = after(pieces[0][0], done)
        return [(held, pieces[0][1])] + pieces[1:]

    def plus(near, arrived):
        return (near + arrived.astype(f32)).astype(bf16)

    (lb4,) = dots(three_b, dens, [(rows_b, (4,), (bf16,))], COST)
    lb = along_z(lb4, -1)
    (ra4,) = dots(later(three_a, lb4), dens, [(rows_a, (4,), (bf16,))], COST)
    ra = along_z(ra4, 1)
    la3, ra3 = dots(later(three_a, ra4), dens, [(rows_a, (5, 3), (bf16, f32))], COST)
    la = along_z(la3, -1)
    rb3, lb3 = dots(later(three_b, la3), dens, [(rows_b, (3, 5), (bf16, f32))], COST)
    rb = along_z(rb3, 1)
    sa = plus(ra3, ra)
    sb = plus(lb3, lb)
    ra, lb = along_z(sa, 1), along_z(sb, -1)
    ra2, la2 = dots(later(three_a, sa), dens, [(rows_a, (2, 6), (f32, f32))])
    rb2, lb2 = dots(later(three_b, sb), dens, [(rows_b, (2, 6), (f32, f32))])
    la, rb = along_z(plus(la2, la), -1), along_z(plus(rb2, rb), 1)
    sa = plus(ra2, ra)
    sb = plus(lb2, lb)
    ra, lb = along_z(sa, 1), along_z(sb, -1)
    ra1, la1 = dots(later(three_a, sa), dens, [(rows_a, (1, 7), (f32, f32))])
    rb1, lb1 = dots(later(three_b, sb), dens, [(rows_b, (1, 7), (f32, f32))])
    la, rb = along_z(plus(la1, la), -1), along_z(plus(rb1, rb), 1)
    sa = plus(ra1, ra)
    sb = plus(lb1, lb)
    ra, lb = along_z(sa, 1), along_z(sb, -1)
    (enda,) = dots(later(three_a, sa), dens, [(rows_a, (0,), (f32,))])
    (endb,) = dots(later(three_b, sb), dens, [(rows_b, (0,), (f32,))])
    top = enda + la.astype(f32) + ra.astype(f32)
    bottom = endb + rb.astype(f32) + lb.astype(f32)
    return jnp.concatenate([top.astype(bf16), bottom.astype(bf16)])


def solution(mesh):
    in_specs = (
        P("col", ("row", "depth")),
        P("col", ("row", "depth")),
        P(("col", "depth"), "row"),
        P(("col", "depth"), "row"),
        P(("row", "depth")),
    )
    out_specs = P("col", ("row", "depth"))
    return jax.shard_map(
        on_device, mesh=mesh, in_specs=in_specs, out_specs=out_specs, check_vma=False
    )
```

```python
import functools

import jax
import jax.numpy as jnp
from jax import lax
from jax.experimental import pallas as pl
from jax.experimental.pallas import tpu as pltpu
from jax.sharding import PartitionSpec as P

BS = 32
COST = 1
AHEAD = 2 * 10**9
VMEM_BYTES = 8 * 1024 * 1024

vmem = functools.partial(pl.BlockSpec, memory_space=pltpu.VMEM)


def call(kernel, outs, operands, in_specs, scratch=(), flops=0, limit=VMEM_BYTES, out_space=pltpu.VMEM, aliases={}):
    return pl.pallas_call(
        kernel,
        out_shape=outs,
        in_specs=in_specs,
        out_specs=[pl.BlockSpec(memory_space=out_space)] * len(outs),
        scratch_shapes=list(scratch),
        input_output_aliases=aliases,
        compiler_params=pltpu.CompilerParams(vmem_limit_bytes=limit),
        cost_estimate=pl.CostEstimate(flops=flops, bytes_accessed=0, transcendentals=0),
    )(*operands)


def masked(three_center, three_mask, density, density_mask, nu_sizes):
    rows, cols = three_center.shape
    deep, wide = density.shape
    share = 128
    count = wide // (2 * share)
    tiles = cols // BS

    def kernel(three_hbm, mask3_hbm, dens_hbm, maskd_hbm, sizes_hbm, live_hbm, own_hbm, other_hbm, *scratch):
        three_ref, mask3_ref, dens_ref, maskd_ref, sizes_ref, held, live_ref, own_ref, other_ref, sems = scratch
        depth = lax.axis_index("depth")
        z, c = depth // 2, depth % 2
        copies = [
            pltpu.make_async_copy(src, dst, sems.at[i])
            for i, (src, dst) in enumerate(
                (
                    (maskd_hbm, maskd_ref),
                    (sizes_hbm, sizes_ref),
                    (mask3_hbm, mask3_ref),
                    (dens_hbm, dens_ref),
                    (three_hbm, three_ref),
                )
            )
        ]
        for copy in copies:
            copy.start()
        lane = lax.broadcasted_iota(jnp.int32, (wide // BS, wide), 1)
        spread = (lane // BS == lax.broadcasted_iota(jnp.int32, lane.shape, 0)).astype(jnp.bfloat16)
        copies[0].wait()
        held[...] = jnp.dot(
            maskd_ref[...].astype(jnp.float32).astype(jnp.bfloat16), spread, preferred_element_type=jnp.float32
        )
        copies[1].wait()
        lane = lax.broadcasted_iota(jnp.int32, (tiles, cols), 1)
        tile = lax.broadcasted_iota(jnp.int32, lane.shape, 0)
        size = jnp.zeros_like(lane)
        for j in range(tiles):
            size = jnp.where(tile == j, sizes_ref[j], size)
        spread = ((lane // BS == tile) & (lane % BS < size)).astype(jnp.bfloat16)
        copies[2].wait()
        keep = lax.dot_general(
            mask3_ref[...].astype(jnp.float32).astype(jnp.bfloat16),
            spread,
            (((0,), (0,)), ((), ())),
            preferred_element_type=jnp.float32,
        )
        copies[3].wait()
        for j in range(count):
            first = lax.rem(z + j, count) * 2
            for side, out_ref in ((c, own_ref), (1 - c, other_ref)):
                place = pl.multiple_of((first + side) * share, share)
                for i in range(deep // BS):
                    kept = jnp.broadcast_to(held[i : i + 1, pl.ds(place, share)], (BS, share)).astype(jnp.bfloat16)
                    piece = dens_ref[i * BS : (i + 1) * BS, pl.ds(place, share)]
                    out_ref[j * deep + i * BS : j * deep + (i + 1) * BS, :] = piece * kept
        leaving = [(other_ref, other_hbm), (own_ref, own_hbm)]
        leaving = [pltpu.make_async_copy(src, dst, sems.at[5 + i]) for i, (src, dst) in enumerate(leaving)]
        for copy in leaving:
            copy.start()
        copies[4].wait()
        part = rows // 2
        for g in range(rows // BS):
            kept = jnp.broadcast_to(keep[g : g + 1, :], (BS, cols)).astype(jnp.bfloat16)
            live_ref[g * BS : (g + 1) * BS, :] = three_ref[g * BS : (g + 1) * BS, :] * kept
            if (g + 1) * BS % part == 0:
                at = pl.ds((g + 1) * BS - part, part)
                copy = pltpu.make_async_copy(live_ref.at[at], live_hbm.at[at], sems.at[6 + (g + 1) * BS // part])
                copy.start()
                leaving.append(copy)
        for copy in leaving:
            copy.wait()

    return call(
        kernel,
        [jax.ShapeDtypeStruct((rows, cols), jnp.bfloat16)]
        + [jax.ShapeDtypeStruct((r, share), jnp.bfloat16) for r in (count * deep, count * deep)],
        (three_center, three_mask.T, density, density_mask, nu_sizes),
        [pl.BlockSpec(memory_space=pltpu.HBM)] * 5,
        [
            pltpu.VMEM((rows, cols), jnp.bfloat16),
            pltpu.VMEM((tiles, rows // BS), jnp.int32),
            pltpu.VMEM((deep, wide), jnp.bfloat16),
            pltpu.VMEM((deep // BS, wide // BS), jnp.int32),
            pltpu.SMEM((tiles,), jnp.int32),
            pltpu.VMEM((deep // BS, wide), jnp.float32),
            pltpu.VMEM((rows, cols), jnp.bfloat16),
            pltpu.VMEM((count * deep, share), jnp.bfloat16),
            pltpu.VMEM((count * deep, share), jnp.bfloat16),
            pltpu.SemaphoreType.DMA((9,)),
        ],
        limit=56 * 1024 * 1024,
        out_space=pltpu.HBM,
    )


def in_order(blocks):
    deep, share = 128, blocks[0].shape[1]
    both = blocks[0].shape[0] // 2
    whole = 2 * len(blocks) * deep

    def kernel(*refs):
        out = refs[-1]
        across = lax.axis_index("col") - lax.axis_index("row")
        turn = jnp.where(lax.axis_index("depth") % 2 == 0, across, -across) + 4
        for s, block in enumerate(refs[:-1]):
            at = pl.multiple_of(lax.rem(s + turn, 4) * (2 * deep), 2 * deep)
            for j in range(both // deep):
                for side in range(2):
                    piece = block[side * both + j * deep : side * both + (j + 1) * deep, :]
                    out[pl.ds(j * whole + side * deep + at, deep), :] = piece

    return call(
        kernel,
        [jax.ShapeDtypeStruct((both // deep * whole, share), blocks[0].dtype)],
        blocks,
        [vmem()] * len(blocks),
        flops=AHEAD,
    )[0]


def dots(three, dens, jobs, cost=0):
    deep, share = 8 * 128, dens.shape[1]
    arrays = []
    for array, _ in three:
        if not any(array is other for other in arrays):
            arrays.append(array)
    three_at = [([array is other for other in arrays].index(True), base) for array, base in three]

    def kernel(*refs):
        ins, dens_ref, outs = refs[: len(arrays)], refs[len(arrays)], list(refs[len(arrays) + 1 :])
        for rows, picked, kinds in jobs:
            right = jnp.concatenate([dens_ref[j * deep : (j + 1) * deep, :] for j in picked], axis=1)
            tile = rows // -(-rows // 512)
            for m in range(0, rows, tile):
                left = jnp.concatenate([ins[w][base + m : base + m + tile, :] for w, base in three_at], axis=1)
                total = jnp.dot(left, right, preferred_element_type=jnp.float32)
                for i, kind in enumerate(kinds):
                    outs[i][m : m + tile, :] = total[:, i * share : (i + 1) * share].astype(kind)
            outs = outs[len(kinds) :]

    return call(
        kernel,
        [jax.ShapeDtypeStruct((rows, share), kind) for rows, _, kinds in jobs for kind in kinds],
        (*arrays, dens),
        [vmem()] * (len(arrays) + 1),
        flops=cost * 2 * deep * share * sum(rows * len(picked) for rows, picked, _ in jobs),
    )


def finished(terms, total, first, result=None):
    rows, share = terms[0].shape
    part = rows // 2

    def kernel(near_ref, right_ref, left_ref, *refs):
        out, held, sems = refs[-3:]
        copies = []
        for i in range(2):
            at = pl.ds(i * part, part)
            added = near_ref[at, :] + right_ref[at, :].astype(jnp.float32) + left_ref[at, :].astype(jnp.float32)
            held[at, :] = added.astype(held.dtype)
            place = pl.ds(first + i * part, part)
            copies.append(pltpu.make_async_copy(held.at[at], out.at[place], sems.at[i]))
            copies[-1].start()
        for copy in copies:
            copy.wait()

    earlier = () if result is None else (result,)
    return call(
        kernel,
        [jax.ShapeDtypeStruct((total, share), jnp.bfloat16)],
        (*terms, *earlier),
        [vmem()] * 3 + [pl.BlockSpec(memory_space=pltpu.HBM)] * len(earlier),
        [pltpu.VMEM((rows, share), jnp.bfloat16), pltpu.SemaphoreType.DMA((2,))],
        out_space=pltpu.HBM,
        aliases={3: 0} if earlier else {},
    )[0]


def along_z(block, distance):
    count = lax.axis_size("depth") // 2
    route = [(z * 2 + c, (z + distance) % count * 2 + c) for z in range(count) for c in range(2)]
    return lax.ppermute(block, "depth", route)


def other_core(block):
    return lax.ppermute(block, "depth", [(i, i ^ 1) for i in range(lax.axis_size("depth"))])


def opposed(block, axis, step):
    count, depth = lax.axis_size(axis), lax.axis_size("depth")
    route = [
        (i * depth + d, (i + (step if d % 2 == 0 else -step)) % count * depth + d)
        for i in range(count)
        for d in range(depth)
    ]
    return lax.ppermute(block, (axis, "depth"), route)


def after(block, *earlier):
    return lax.optimization_barrier((block, *earlier))[0]


def on_device(three_center, three_mask, density, density_mask, nu_sizes):
    live, own, other = masked(three_center, three_mask, density, density_mask, nu_sizes)
    bf16, f32 = jnp.bfloat16, jnp.float32
    n, deep = live.shape[0], 128
    rows_a = n * 16 // 32
    rows_b = n - rows_a

    a_back = opposed(live, "row", 1)
    dens = jnp.concatenate([own, other_core(other)])
    b_back = opposed(dens, "col", 1)
    a_front, b_front = opposed(live, "row", -1), opposed(dens, "col", -1)
    live_other = other_core(live)
    a_far, b_far = opposed(a_back, "row", 1), opposed(b_back, "col", 1)
    back_other = other_core(a_back)
    a_front, b_front, live_other = lax.optimization_barrier((a_front, b_front, live_other))
    front_other = other_core(a_front)
    far_other = other_core(a_far)

    def three(at):
        return [
            (x, at) for x in (live, live_other, a_front, back_other, a_far, far_other, a_back, front_other)
        ]

    three_a, three_b = three(0), three(rows_a)
    dens = in_order((dens, b_front, b_far, b_back))

    def later(pieces, done):
        held = after(pieces[0][0], done)
        return [(held, pieces[0][1])] + pieces[1:]

    def plus(near, arrived):
        return (near + arrived.astype(f32)).astype(bf16)

    (lb4,) = dots(three_b, dens, [(rows_b, (4,), (bf16,))], COST)
    lb = along_z(lb4, -1)
    (ra4,) = dots(later(three_a, lb4), dens, [(rows_a, (4,), (bf16,))], COST)
    ra = along_z(ra4, 1)
    la3, ra3 = dots(later(three_a, ra4), dens, [(rows_a, (5, 3), (bf16, f32))], COST)
    la = along_z(la3, -1)
    rb3, lb3 = dots(later(three_b, la3), dens, [(rows_b, (3, 5), (bf16, f32))], COST)
    rb = along_z(rb3, 1)
    sa = plus(ra3, ra)
    sb = plus(lb3, lb)
    ra, lb = along_z(sa, 1), along_z(sb, -1)
    ra2, la2 = dots(later(three_a, sa), dens, [(rows_a, (2, 6), (f32, f32))])
    rb2, lb2 = dots(later(three_b, sb), dens, [(rows_b, (2, 6), (f32, f32))])
    la, rb = along_z(plus(la2, la), -1), along_z(plus(rb2, rb), 1)
    sa = plus(ra2, ra)
    sb = plus(lb2, lb)
    ra, lb = along_z(sa, 1), along_z(sb, -1)
    ra1, la1 = dots(later(three_a, sa), dens, [(rows_a, (1, 7), (f32, f32))])
    rb1, lb1 = dots(later(three_b, sb), dens, [(rows_b, (1, 7), (f32, f32))])
    la, rb = along_z(plus(la1, la), -1), along_z(plus(rb1, rb), 1)
    sa = plus(ra1, ra)
    sb = plus(lb1, lb)
    ra, lb = along_z(sa, 1), along_z(sb, -1)
    (enda,) = dots(later(three_a, sa), dens, [(rows_a, (0,), (f32,))])
    (endb,) = dots(later(three_b, sb), dens, [(rows_b, (0,), (f32,))])
    lower = finished((endb, rb, lb), n, rows_a)
    return finished((enda, ra, la), n, 0, lower)


def solution(mesh):
    in_specs = (
        P("col", ("row", "depth")),
        P("col", ("row", "depth")),
        P(("col", "depth"), "row"),
        P(("col", "depth"), "row"),
        P(("row", "depth")),
    )
    out_specs = P("col", ("row", "depth"))
    return jax.shard_map(
        on_device, mesh=mesh, in_specs=in_specs, out_specs=out_specs, check_vma=False
    )
```
